32 devices in a mesh: orbit: 2 (over x), seg: 8 (over z, y), tile: 2 (over core).
Axes of the slice: x: 2, y: 2, z: 4, core: 2. Of those that a mesh axis runs over, the one named last changes fastest.
Arguments:
- base: float32 [16, 2, 64, 4096], P(('orbit', 'seg'), None, 'tile'), parts along dimension 0, may hold values from -6 to 6
- direction: float32 [16, 2, 64, 4096], P(('orbit', 'seg'), None, 'tile'), parts along dimension 0, may hold values from -6 to 6
- step_time: float32 [2], P('orbit'), parts along dimension 0, may hold values from 0.05 to 0.15
- step_change: float32 [2], P('orbit'), parts along dimension 0, may hold values from -0.6 to 0.6
Outputs:
- grad_state: float32 [16, 2, 64, 4096], P(('orbit', 'seg'), None, 'tile'), parts along dimension 0
- grad_step: float32 [2], P('orbit'), parts along dimension 0
- residual_ms: float32 [2], P('orbit'), parts along dimension 0
The draws below stay inside these ranges and needn't reach their ends.
There are 2 independent parts, one for each index of `orbit`. The reference program is written for one: setup_inputs(seed, part) draws one part's arguments, and reference() takes and returns one part's arrays. A program takes and returns all parts, laid end to end along the dimension named above; each array names one. Nothing has to cross between parts.
All inputs are finite; a program needn't handle non-finite values.
Results may differ from the reference program's by a relative error of at most 0.00002.
Values sent between devices are 32-bit elements; how exact they have to be, the bound alone decides.
A program may use at most 64 MiB of HBM per device.

```python
import math
import jax
import jax.numpy as jnp
from jax import lax

COLS = 4096
K_FORCE = 4
ROWS = 64
SEGMENTS = 8


def levels(rng, extent, split, least, high):
    gain = 1.0
    for axis_at, parts in split:
        steps = jax.random.uniform(jax.random.fold_in(jax.random.fold_in(rng, 6), axis_at), (parts,), jnp.float32, least / len(split), high / len(split))
        gain = gain * jnp.repeat(jnp.exp(steps), extent[axis_at] // parts).reshape((-1,) + (1,) * (len(extent) - 1 - axis_at))
    return gain


def bell_draw(key, shape, width, reach, split=(), held_as=jnp.bfloat16):
    entries = width * jax.random.normal(key, shape, jnp.float32)
    if split:
        entries = entries * levels(key, shape, split, -0.22, 0.18)
    return jnp.clip(entries, -reach, reach).astype(held_as)


def setup_inputs(seed: int = 0, part: int = 0) -> dict:
    key_of = jax.random.split(jax.random.key(seed), 5)
    part_keys = jax.random.split(jax.random.fold_in(key_of[4], part), 5)
    base = bell_draw(part_keys[0], (SEGMENTS, 2, ROWS, COLS), 1.0, 6.0, ((0, 8), (2, 2)), jnp.float32)
    direction = bell_draw(part_keys[1], (SEGMENTS, 2, ROWS, COLS), 1.0, 6.0, ((0, 8), (2, 2)), jnp.float32)
    step_time = jnp.clip(jnp.exp(jax.random.uniform(part_keys[2], (1,), jnp.float32, math.log(0.05), math.log(0.15))), 0.05, 0.15)
    step_change = bell_draw(part_keys[3], (1,), 0.1, 0.6, (), jnp.float32)
    return {"base": base, "direction": direction, "step_time": step_time, "step_change": step_change}


VISC = 0.5


def rows_diff(wide):
    return (wide[..., 2:, :] - wide[..., :-2, :]) * 0.5


def cols_diff(inner):
    return (jnp.roll(inner, -1, -1) - jnp.roll(inner, 1, -1)) * 0.5


def laplace(wide):
    inner = wide[..., 1:-1, :]
    return wide[..., 2:, :] + wide[..., :-2, :] + jnp.roll(inner, -1, -1) + jnp.roll(inner, 1, -1) - 4.0 * inner


def rate(base_wide, forcing):
    inner = base_wide[:, 1:-1, :]
    value = -(inner[0] * rows_diff(base_wide) + inner[1] * cols_diff(inner)) + VISC * laplace(base_wide)
    push = jnp.stack([jnp.broadcast_to(forcing, inner.shape[1:]), jnp.zeros(inner.shape[1:], jnp.float32)])
    return value + push


def tangent(base_wide, pert_wide, substep):
    base_in = base_wide[:, 1:-1, :]
    pert_in = pert_wide[:, 1:-1, :]
    grad_bx = rows_diff(base_wide)
    grad_by = cols_diff(base_in)
    change = -base_in[0] * rows_diff(pert_wide) - base_in[1] * cols_diff(pert_in)
    change = change - pert_in[0] * grad_bx - pert_in[1] * grad_by + VISC * laplace(pert_wide)
    return pert_in + substep * change


def adjoint(base_wide, costate_wide, substep):
    base_in = base_wide[:, 1:-1, :]
    cost_in = costate_wide[:, 1:-1, :]
    flux_x = rows_diff(base_wide[0][None] * costate_wide)
    flux_y = cols_diff(base_in[1][None] * cost_in)
    grad_bx = rows_diff(base_wide)
    grad_by = cols_diff(base_in)
    cross = jnp.stack([grad_bx[0] * cost_in[0] + grad_bx[1] * cost_in[1],
                       grad_by[0] * cost_in[0] + grad_by[1] * cost_in[1]])
    return cost_in + substep * (flux_x + flux_y + VISC * laplace(costate_wide) - cross)


def wrap_rows(field):
    return jnp.concatenate([field[:, -1:, :], field, field[:, :1, :]], axis=1)


def reference(base, direction, step_time, step_change):
    substep = step_time[0]
    change = step_change[0]
    forcing = jnp.sin(2.0 * math.pi * K_FORCE * jnp.arange(COLS, dtype=jnp.float32) / COLS)

    def forward(pair):
        start, pert = pair
        start_wide = wrap_rows(start)
        rate_zero = rate(start_wide, forcing)
        middle = start + substep * rate_zero
        pert_one = tangent(start_wide, wrap_rows(pert), substep) + change * rate_zero
        middle_wide = wrap_rows(middle)
        return tangent(middle_wide, wrap_rows(pert_one), substep) + change * rate(middle_wide, forcing)

    ends = lax.map(forward, (base, direction))
    resid = ends - jnp.roll(direction, -1, axis=0)
    behind = jnp.roll(resid, 1, axis=0)

    def backward(pair):
        start, res = pair
        start_wide = wrap_rows(start)
        rate_zero = rate(start_wide, forcing)
        middle = start + substep * rate_zero
        middle_wide = wrap_rows(middle)
        rate_one = rate(middle_wide, forcing)
        adj_one = adjoint(middle_wide, wrap_rows(res), substep)
        adj_zero = adjoint(start_wide, wrap_rows(adj_one), substep)
        return adj_zero, jnp.sum(rate_zero * adj_one) + jnp.sum(rate_one * res)

    adj_all, terms = lax.map(backward, (base, resid))
    grad_state = adj_all - behind
    grad_step = (jnp.sum(terms) / (ROWS * COLS * SEGMENTS)).reshape(1)
    residual_ms = (jnp.sum(resid * resid) / (2 * ROWS * COLS * SEGMENTS)).reshape(1)
    return grad_state, grad_step, residual_ms
```

```python
import functools
import math

import jax
import jax.numpy as jnp
import numpy as np
from jax import lax
from jax.experimental import pallas as pl
from jax.experimental.pallas import tpu as pltpu
from jax.sharding import PartitionSpec as P

K_FORCE = 4

VISC = 0.5

MESH = pl.DeviceIdType.MESH
LANES = 128
SUB = 8
CHUNK = 256


class Window:
    def __init__(self, ref, comp, col, width):
        full, rows = ref.shape[-1], ref.shape[-2] - 2 * SUB
        here = pl.ds(pl.multiple_of(col, LANES), width)
        before = pl.multiple_of(lax.rem(col + (full - LANES), full), LANES)
        after = pl.multiple_of(lax.rem(col + width, full), LANES)
        own = pl.ds(SUB, rows)
        self.mid = ref[comp, own, here]
        self.up = ref[comp, pl.ds(SUB - 1, rows), here]
        self.down = ref[comp, pl.ds(SUB + 1, rows), here]
        wide = jnp.concatenate(
            [ref[comp, own, pl.ds(before, LANES)], self.mid, ref[comp, own, pl.ds(after, LANES)]], axis=1
        )
        self.left = pltpu.roll(wide, 1, 1)[:, LANES : LANES + width]
        self.right = pltpu.roll(wide, wide.shape[1] - 1, 1)[:, LANES : LANES + width]

    def dx(self):
        return (self.down - self.up) * 0.5

    def dy(self):
        return (self.right - self.left) * 0.5

    def lap(self):
        return self.down + self.up + self.right + self.left - 4.0 * self.mid


def windows(ref, col, width):
    return Window(ref, 0, col, width), Window(ref, 1, col, width)


def rate_and_tangent(b, p, forcing, substep, change):
    rates, images = [], []
    for c in range(2):
        gx, gy = b[c].dx(), b[c].dy()
        rate = -(b[0].mid * gx + b[1].mid * gy) + VISC * b[c].lap()
        if c == 0:
            rate = rate + forcing
        move = -b[0].mid * p[c].dx() - b[1].mid * p[c].dy() - p[0].mid * gx - p[1].mid * gy
        move = move + VISC * p[c].lap()
        rates.append(rate)
        images.append(p[c].mid + substep * move + change * rate)
    return rates, images


def adjoint(b, q, substep):
    outs = []
    for c in range(2):
        flux_x = (b[0].down * q[c].down - b[0].up * q[c].up) * 0.5
        flux_y = (b[1].right * q[c].right - b[1].left * q[c].left) * 0.5
        if c == 0:
            cross = b[0].dx() * q[0].mid + b[1].dx() * q[1].mid
        else:
            cross = b[0].dy() * q[0].mid + b[1].dy() * q[1].mid
        outs.append(q[c].mid + substep * (flux_x + flux_y + VISC * q[c].lap() - cross))
    return outs


def folded(x):
    total = None
    for i in range(x.shape[0] // SUB):
        for k in range(x.shape[1] // LANES):
            part = x[i * SUB : (i + 1) * SUB, k * LANES : (k + 1) * LANES]
            total = part if total is None else total + part
    return total


def kernel(
    n_seg, n_tile, scale_time, scale_square,
    base_hbm, pert_hbm, time_ref, change_ref, force_ref,
    grad_ref, step_ref, square_ref,
    base, pert, mid, pone, res, adj, rate0, rate1, image, ahead, behind, sums, pair, slots,
    local_sem, edge_send, edge_recv, ahead_send, ahead_recv, behind_send, behind_recv,
    pair_sem, slot_send, slot_recv,
):
    seg = lax.axis_index("seg")
    tile = lax.axis_index("tile")
    seg_next, seg_prev = lax.rem(seg + 1, n_seg), lax.rem(seg + n_seg - 1, n_seg)
    tile_next, tile_prev = lax.rem(tile + 1, n_tile), lax.rem(tile + n_tile - 1, n_tile)
    rows, width = pert_hbm.shape[2], pert_hbm.shape[3]
    blocks = rows // SUB
    chunk = min(CHUNK, width)
    substep, change = time_ref[0], change_ref[0]

    barrier = pltpu.get_barrier_semaphore()
    for k in range(1, n_seg):
        pl.semaphore_signal(barrier, inc=1, device_id={"seg": lax.rem(seg + k, n_seg)}, device_id_type=MESH)
    for k in range(1, n_tile):
        pl.semaphore_signal(barrier, inc=1, device_id={"tile": lax.rem(tile + k, n_tile)}, device_id_type=MESH)

    own = pl.ds(SUB, rows)
    loads = [
        pltpu.make_async_copy(base_hbm.at[0], base.at[:, own, :], local_sem.at[0]),
        pltpu.make_async_copy(pert_hbm.at[0], pert.at[:, own, :], local_sem.at[1]),
    ]
    for copy in loads:
        copy.start()
    pl.semaphore_wait(barrier, n_seg - 1 + n_tile - 1)

    def edges(first, last, field, at):
        down = pltpu.make_async_remote_copy(
            src_ref=last, dst_ref=field.at[:, pl.ds(0, SUB), :], send_sem=edge_send.at[at], recv_sem=edge_recv.at[at],
            device_id={"tile": tile_next}, device_id_type=MESH)
        up = pltpu.make_async_remote_copy(
            src_ref=first, dst_ref=field.at[:, pl.ds(SUB + rows, SUB), :], send_sem=edge_send.at[at + 1],
            recv_sem=edge_recv.at[at + 1], device_id={"tile": tile_prev}, device_id_type=MESH)
        down.start()
        up.start()
        return [down, up]

    def field_edges(field, at):
        return edges(field.at[:, pl.ds(SUB, SUB), :], field.at[:, pl.ds(rows, SUB), :], field, at)

    def hbm_edges(field_hbm, field, at):
        return edges(field_hbm.at[0, :, pl.ds(0, SUB), :], field_hbm.at[0, :, pl.ds(rows - SUB, SUB), :], field, at)

    pending = hbm_edges(base_hbm, base, 0) + hbm_edges(pert_hbm, pert, 2)
    aheads = []
    for k in range(blocks):
        part = pl.ds(k * SUB, SUB)
        copy = pltpu.make_async_remote_copy(
            src_ref=pert_hbm.at[0, :, part, :], dst_ref=ahead.at[:, part, :], send_sem=ahead_send.at[k],
            recv_sem=ahead_recv.at[k], device_id={"seg": seg_prev}, device_id_type=MESH)
        copy.start()
        aheads.append(copy)

    def sweep(step):
        def one(j, _):
            step(pl.multiple_of(j * chunk, chunk))
            return 0

        lax.fori_loop(0, width // chunk, one, 0)

    sums[...] = jnp.zeros_like(sums)
    for copy in loads:
        copy.wait()
    for copy in pending:
        copy.wait()

    def first_step(col):
        b, p = windows(base, col, chunk), windows(pert, col, chunk)
        forcing = force_ref[:, pl.ds(col, chunk)]
        rates, images = rate_and_tangent(b, p, forcing, substep, change)
        for c in range(2):
            rate0[c, :, pl.ds(col, chunk)] = rates[c]
            mid[c, own, pl.ds(col, chunk)] = b[c].mid + substep * rates[c]
            pone[c, own, pl.ds(col, chunk)] = images[c]

    sweep(first_step)
    for copy in field_edges(mid, 4) + field_edges(pone, 6):
        copy.wait()

    def second_step(col):
        b, p = windows(mid, col, chunk), windows(pone, col, chunk)
        forcing = force_ref[:, pl.ds(col, chunk)]
        rates, images = rate_and_tangent(b, p, forcing, substep, change)
        for c in range(2):
            rate1[c, :, pl.ds(col, chunk)] = rates[c]
            image[c, :, pl.ds(col, chunk)] = images[c]

    sweep(second_step)
    for copy in aheads:
        copy.wait_send()
    behinds = []
    for k in range(blocks):
        part = pl.ds(k * SUB, SUB)
        copy = pltpu.make_async_remote_copy(
            src_ref=image.at[:, part, :], dst_ref=behind.at[:, part, :], send_sem=behind_send.at[k],
            recv_sem=behind_recv.at[k], device_id={"seg": seg_next}, device_id_type=MESH)
        copy.start()
        behinds.append(copy)

    for k in range(blocks):
        aheads[k].wait_recv()
        part, wide_part = pl.ds(k * SUB, SUB), pl.ds((k + 1) * SUB, SUB)

        def residual_step(col):
            for c in range(2):
                value = image[c, part, pl.ds(col, chunk)] - ahead[c, part, pl.ds(col, chunk)]
                res[c, wide_part, pl.ds(col, chunk)] = value
                sums[0] += folded(value * value)
                sums[1] += folded(rate1[c, part, pl.ds(col, chunk)] * value)

        sweep(residual_step)
    for copy in field_edges(res, 8):
        copy.wait()

    def adjoint_one(col):
        outs = adjoint(windows(mid, col, chunk), windows(res, col, chunk), substep)
        for c in range(2):
            adj[c, own, pl.ds(col, chunk)] = outs[c]
            sums[1] += folded(rate0[c, :, pl.ds(col, chunk)] * outs[c])

    sweep(adjoint_one)
    pending = field_edges(adj, 10)
    shares = []
    for k in range(1, n_tile):
        copy = pltpu.make_async_remote_copy(
            src_ref=sums, dst_ref=pair.at[tile], send_sem=pair_sem.at[0, k], recv_sem=pair_sem.at[1, tile],
            device_id={"tile": lax.rem(tile + k, n_tile)}, device_id_type=MESH)
        copy.start()
        shares.append(copy)
    for copy in pending:
        copy.wait()

    def adjoint_zero(col):
        outs = adjoint(windows(base, col, chunk), windows(adj, col, chunk), substep)
        for c in range(2):
            pone[c, own, pl.ds(col, chunk)] = outs[c] + pert[c, own, pl.ds(col, chunk)]

    sweep(adjoint_zero)

    for copy in shares:
        copy.wait_send()
    for k in range(1, n_tile):
        source = lax.rem(tile + k, n_tile)
        pltpu.make_async_remote_copy(
            src_ref=sums, dst_ref=pair.at[source], send_sem=pair_sem.at[0, k], recv_sem=pair_sem.at[1, source],
            device_id={"tile": source}, device_id_type=MESH).wait_recv()
    pair[tile] = sums[...]
    both = pair[0]
    for k in range(1, n_tile):
        both = both + pair[k]
    slots[seg] = both
    sends = []
    for k in range(1, n_seg):
        copy = pltpu.make_async_remote_copy(
            src_ref=slots.at[seg], dst_ref=slots.at[seg], send_sem=slot_send.at[k], recv_sem=slot_recv.at[seg],
            device_id={"seg": lax.rem(seg + k, n_seg)}, device_id_type=MESH)
        copy.start()
        sends.append(copy)
    for copy in sends:
        copy.wait_send()
    for k in range(1, n_seg):
        source = lax.rem(seg + k, n_seg)
        pltpu.make_async_remote_copy(
            src_ref=slots.at[source], dst_ref=slots.at[source], send_sem=slot_send.at[k],
            recv_sem=slot_recv.at[source], device_id={"seg": source}, device_id_type=MESH).wait_recv()
    total = slots[0]
    for k in range(1, n_seg):
        total = total + slots[k]
    square_ref[0] = jnp.sum(total[0]) * scale_square
    step_ref[0] = jnp.sum(total[1]) * scale_time

    for k in range(blocks):
        behinds[k].wait_recv()
        part, wide_part = pl.ds(k * SUB, SUB), pl.ds((k + 1) * SUB, SUB)

        def last_step(col):
            for c in range(2):
                here = pl.ds(col, chunk)
                grad_ref[0, c, part, here] = pone[c, wide_part, here] - behind[c, part, here]

        sweep(last_step)
    for copy in behinds:
        copy.wait_send()


def body(n_seg, n_tile, base, direction, step_time, step_change):
    _, comps, rows, width = base.shape
    cells = rows * width * n_seg * n_tile
    forcing = np.sin(2.0 * math.pi * K_FORCE * np.arange(width) / width).astype(np.float32)[None]
    blocks = rows // SUB
    wide = pltpu.VMEM((comps, rows + 2 * SUB, width), jnp.float32)
    plain = pltpu.VMEM((comps, rows, width), jnp.float32)
    part = (2, SUB, LANES)
    dma = pltpu.SemaphoreType.DMA
    anywhere = pl.BlockSpec(memory_space=pl.ANY)
    scalar = pl.BlockSpec(memory_space=pltpu.SMEM)
    vector = pl.BlockSpec(memory_space=pltpu.VMEM)
    one = jax.ShapeDtypeStruct((1,), jnp.float32)
    return pl.pallas_call(
        functools.partial(kernel, n_seg, n_tile, 1.0 / cells, 1.0 / (2 * cells)),
        out_shape=(jax.ShapeDtypeStruct(base.shape, jnp.float32), one, one),
        in_specs=[anywhere, anywhere, scalar, scalar, vector],
        out_specs=(vector, scalar, scalar),
        scratch_shapes=[wide] * 6 + [plain] * 5 + [
            pltpu.VMEM(part, jnp.float32),
            pltpu.VMEM((n_tile, *part), jnp.float32),
            pltpu.VMEM((n_seg, *part), jnp.float32),
            dma((2,)), dma((12,)), dma((12,)), dma((blocks,)), dma((blocks,)), dma((blocks,)), dma((blocks,)),
            dma((2, n_tile)), dma((n_seg,)), dma((n_seg,)),
        ],
        compiler_params=pltpu.CompilerParams(
            collective_id=0, has_side_effects=True, vmem_limit_bytes=40 * 1024 * 1024
        ),
    )(base, direction, step_time, step_change, forcing)


def solution(mesh):
    spec = P(("orbit", "seg"), None, "tile", None)
    return jax.shard_map(
        functools.partial(body, mesh.shape["seg"], mesh.shape["tile"]),
        mesh=mesh,
        in_specs=(spec, spec, P("orbit"), P("orbit")),
        out_specs=(spec, P("orbit"), P("orbit")),
        check_vma=False,
    )
```

```python
import functools
import math

import jax
import jax.numpy as jnp
import numpy as np
from jax import lax
from jax.experimental import pallas as pl
from jax.experimental.pallas import tpu as pltpu
from jax.sharding import PartitionSpec as P

K_FORCE = 4

VISC = 0.5

MESH = pl.DeviceIdType.MESH
LANES = 128
SUB = 8
CHUNK = 256


class Window:
    def __init__(self, ref, comp, col, width):
        full, rows = ref.shape[-1], ref.shape[-2] - 2 * SUB
        here = pl.ds(pl.multiple_of(col, LANES), width)
        before = pl.multiple_of(lax.rem(col + (full - LANES), full), LANES)
        after = pl.multiple_of(lax.rem(col + width, full), LANES)
        own = pl.ds(SUB, rows)
        self.mid = ref[comp, own, here]
        self.up = ref[comp, pl.ds(SUB - 1, rows), here]
        self.down = ref[comp, pl.ds(SUB + 1, rows), here]
        wide = jnp.concatenate(
            [ref[comp, own, pl.ds(before, LANES)], self.mid, ref[comp, own, pl.ds(after, LANES)]], axis=1
        )
        self.left = pltpu.roll(wide, 1, 1)[:, LANES : LANES + width]
        self.right = pltpu.roll(wide, wide.shape[1] - 1, 1)[:, LANES : LANES + width]

    def dx(self):
        return (self.down - self.up) * 0.5

    def dy(self):
        return (self.right - self.left) * 0.5

    def lap(self):
        return self.down + self.up + self.right + self.left - 4.0 * self.mid


def windows(ref, col, width):
    return Window(ref, 0, col, width), Window(ref, 1, col, width)


def rate_and_tangent(b, p, forcing, substep, change):
    rates, images = [], []
    for c in range(2):
        gx, gy = b[c].dx(), b[c].dy()
        rate = -(b[0].mid * gx + b[1].mid * gy) + VISC * b[c].lap()
        if c == 0:
            rate = rate + forcing
        move = -b[0].mid * p[c].dx() - b[1].mid * p[c].dy() - p[0].mid * gx - p[1].mid * gy
        move = move + VISC * p[c].lap()
        rates.append(rate)
        images.append(p[c].mid + substep * move + change * rate)
    return rates, images


def adjoint(b, q, substep):
    outs = []
    for c in range(2):
        flux_x = (b[0].down * q[c].down - b[0].up * q[c].up) * 0.5
        flux_y = (b[1].right * q[c].right - b[1].left * q[c].left) * 0.5
        if c == 0:
            cross = b[0].dx() * q[0].mid + b[1].dx() * q[1].mid
        else:
            cross = b[0].dy() * q[0].mid + b[1].dy() * q[1].mid
        outs.append(q[c].mid + substep * (flux_x + flux_y + VISC * q[c].lap() - cross))
    return outs


def folded(x):
    total = None
    for i in range(x.shape[0] // SUB):
        for k in range(x.shape[1] // LANES):
            part = x[i * SUB : (i + 1) * SUB, k * LANES : (k + 1) * LANES]
            total = part if total is None else total + part
    return total


def kernel(
    n_seg, n_tile, scale_time, scale_square,
    base_hbm, pert_hbm, time_ref, change_ref, force_hbm,
    grad_ref, step_ref, square_ref,
    base, pert, mid, pone, res, adj, rate0, rate1, image, ahead, behind, sums, pair, slots, force_ref,
    local_sem, edge_send, edge_recv, ahead_send, ahead_recv, behind_send, behind_recv,
    pair_sem, slot_send, slot_recv,
):
    seg = lax.axis_index("seg")
    tile = lax.axis_index("tile")
    seg_next, seg_prev = lax.rem(seg + 1, n_seg), lax.rem(seg + n_seg - 1, n_seg)
    tile_next, tile_prev = lax.rem(tile + 1, n_tile), lax.rem(tile + n_tile - 1, n_tile)
    rows, width = pert_hbm.shape[2], pert_hbm.shape[3]
    blocks = rows // SUB
    chunk = min(CHUNK, width)
    substep, change = time_ref[0], change_ref[0]

    barrier = pltpu.get_barrier_semaphore()
    for k in range(1, n_seg):
        pl.semaphore_signal(barrier, inc=1, device_id={"seg": lax.rem(seg + k, n_seg)}, device_id_type=MESH)
    for k in range(1, n_tile):
        pl.semaphore_signal(barrier, inc=1, device_id={"tile": lax.rem(tile + k, n_tile)}, device_id_type=MESH)

    own = pl.ds(SUB, rows)
    loads = [
        pltpu.make_async_copy(base_hbm.at[0], base.at[:, own, :], local_sem.at[0]),
        pltpu.make_async_copy(force_hbm, force_ref, local_sem.at[2]),
        pltpu.make_async_copy(pert_hbm.at[0], pert.at[:, own, :], local_sem.at[1]),
    ]
    for copy in loads:
        copy.start()
    pl.semaphore_wait(barrier, n_seg - 1 + n_tile - 1)

    def edges(first, last, field, at):
        down = pltpu.make_async_remote_copy(
            src_ref=last, dst_ref=field.at[:, pl.ds(SUB - 1, 1), :], send_sem=edge_send.at[at], recv_sem=edge_recv.at[at],
            device_id={"tile": tile_next}, device_id_type=MESH)
        up = pltpu.make_async_remote_copy(
            src_ref=first, dst_ref=field.at[:, pl.ds(SUB + rows, 1), :], send_sem=edge_send.at[at + 1],
            recv_sem=edge_recv.at[at + 1], device_id={"tile": tile_prev}, device_id_type=MESH)
        down.start()
        up.start()
        return [down, up]

    def field_edges(field, at):
        return edges(field.at[:, pl.ds(SUB, 1), :], field.at[:, pl.ds(SUB + rows - 1, 1), :], field, at)

    def hbm_edges(field_hbm, field, at):
        return edges(field_hbm.at[0, :, pl.ds(0, 1), :], field_hbm.at[0, :, pl.ds(rows - 1, 1), :], field, at)

    pending = hbm_edges(base_hbm, base, 0) + hbm_edges(pert_hbm, pert, 2)
    aheads = []
    for k in range(blocks):
        part = pl.ds(k * SUB, SUB)
        copy = pltpu.make_async_remote_copy(
            src_ref=pert_hbm.at[0, :, part, :], dst_ref=ahead.at[:, part, :], send_sem=ahead_send.at[k],
            recv_sem=ahead_recv.at[k], device_id={"seg": seg_prev}, device_id_type=MESH)
        if k < blocks // 2:
            copy.start()
        aheads.append(copy)

    def sweep(step):
        def one(j, _):
            step(pl.multiple_of(j * chunk, chunk))
            return 0

        lax.fori_loop(0, width // chunk, one, 0)

    sums[...] = jnp.zeros_like(sums)
    for copy in loads:
        copy.wait()
    for copy in pending:
        copy.wait()

    def first_step(col):
        b, p = windows(base, col, chunk), windows(pert, col, chunk)
        forcing = force_ref[:, pl.ds(col, chunk)]
        rates, images = rate_and_tangent(b, p, forcing, substep, change)
        for c in range(2):
            rate0[c, :, pl.ds(col, chunk)] = rates[c]
            mid[c, own, pl.ds(col, chunk)] = b[c].mid + substep * rates[c]
            pone[c, own, pl.ds(col, chunk)] = images[c]

    sweep(first_step)
    pending = field_edges(mid, 4) + field_edges(pone, 6)
    for copy in aheads[blocks // 2 :]:
        copy.start()
    for copy in pending:
        copy.wait()

    def second_step(col):
        b, p = windows(mid, col, chunk), windows(pone, col, chunk)
        forcing = force_ref[:, pl.ds(col, chunk)]
        rates, images = rate_and_tangent(b, p, forcing, substep, change)
        for c in range(2):
            rate1[c, :, pl.ds(col, chunk)] = rates[c]
            image[c, :, pl.ds(col, chunk)] = images[c]

    sweep(second_step)
    behinds = []
    for k in range(blocks):
        part = pl.ds(k * SUB, SUB)
        copy = pltpu.make_async_remote_copy(
            src_ref=image.at[:, part, :], dst_ref=behind.at[:, part, :], send_sem=behind_send.at[k],
            recv_sem=behind_recv.at[k], device_id={"seg": seg_next}, device_id_type=MESH)
        behinds.append(copy)
    behinds[0].start()

    for k in range(blocks):
        aheads[k].wait_recv()
        part, wide_part = pl.ds(k * SUB, SUB), pl.ds((k + 1) * SUB, SUB)

        def residual_step(col):
            for c in range(2):
                value = image[c, part, pl.ds(col, chunk)] - ahead[c, part, pl.ds(col, chunk)]
                res[c, wide_part, pl.ds(col, chunk)] = value
                sums[0] += folded(value * value)
                sums[1] += folded(rate1[c, part, pl.ds(col, chunk)] * value)

        sweep(residual_step)
    pending = field_edges(res, 8)
    quarter = max(blocks // 4, 1)
    for copy in behinds[1 : 2 * quarter]:
        copy.start()
    for copy in pending + aheads:
        copy.wait_send()
    for copy in pending:
        copy.wait_recv()

    def adjoint_one(col):
        outs = adjoint(windows(mid, col, chunk), windows(res, col, chunk), substep)
        for c in range(2):
            adj[c, own, pl.ds(col, chunk)] = outs[c]
            sums[1] += folded(rate0[c, :, pl.ds(col, chunk)] * outs[c])

    sweep(adjoint_one)
    pending = field_edges(adj, 10)
    shares = []
    for k in range(1, n_tile):
        copy = pltpu.make_async_remote_copy(
            src_ref=sums, dst_ref=pair.at[tile], send_sem=pair_sem.at[0, k], recv_sem=pair_sem.at[1, tile],
            device_id={"tile": lax.rem(tile + k, n_tile)}, device_id_type=MESH)
        copy.start()
        shares.append(copy)
    for copy in behinds[2 * quarter : 3 * quarter]:
        copy.start()
    for copy in pending:
        copy.wait()

    for copy in shares:
        copy.wait_send()
    for k in range(1, n_tile):
        source = lax.rem(tile + k, n_tile)
        pltpu.make_async_remote_copy(
            src_ref=sums, dst_ref=pair.at[source], send_sem=pair_sem.at[0, k], recv_sem=pair_sem.at[1, source],
            device_id={"tile": source}, device_id_type=MESH).wait_recv()
    pair[tile] = sums[...]
    both = pair[0]
    for k in range(1, n_tile):
        both = both + pair[k]
    slots[seg] = both
    sends = []
    for k in range(1, n_seg):
        copy = pltpu.make_async_remote_copy(
            src_ref=slots.at[seg], dst_ref=slots.at[seg], send_sem=slot_send.at[k], recv_sem=slot_recv.at[seg],
            device_id={"seg": lax.rem(seg + k, n_seg)}, device_id_type=MESH)
        copy.start()
        sends.append(copy)
    for copy in behinds[3 * quarter :]:
        copy.start()

    def adjoint_zero(col):
        outs = adjoint(windows(base, col, chunk), windows(adj, col, chunk), substep)
        for c in range(2):
            pone[c, own, pl.ds(col, chunk)] = outs[c] + pert[c, own, pl.ds(col, chunk)]

    sweep(adjoint_zero)

    for copy in sends:
        copy.wait_send()
    for k in range(1, n_seg):
        source = lax.rem(seg + k, n_seg)
        pltpu.make_async_remote_copy(
            src_ref=slots.at[source], dst_ref=slots.at[source], send_sem=slot_send.at[k],
            recv_sem=slot_recv.at[source], device_id={"seg": source}, device_id_type=MESH).wait_recv()
    total = slots[0]
    for k in range(1, n_seg):
        total = total + slots[k]
    square_ref[0] = jnp.sum(total[0]) * scale_square
    step_ref[0] = jnp.sum(total[1]) * scale_time

    for k in range(blocks):
        behinds[k].wait_recv()
        part, wide_part = pl.ds(k * SUB, SUB), pl.ds((k + 1) * SUB, SUB)

        def last_step(col):
            for c in range(2):
                here = pl.ds(col, chunk)
                grad_ref[0, c, part, here] = pone[c, wide_part, here] - behind[c, part, here]

        sweep(last_step)
    for copy in behinds:
        copy.wait_send()


def body(n_seg, n_tile, base, direction, step_time, step_change):
    _, comps, rows, width = base.shape
    cells = rows * width * n_seg * n_tile
    forcing = np.sin(2.0 * math.pi * K_FORCE * np.arange(width) / width).astype(np.float32)[None]
    blocks = rows // SUB
    wide = pltpu.VMEM((comps, rows + 2 * SUB, width), jnp.float32)
    plain = pltpu.VMEM((comps, rows, width), jnp.float32)
    part = (2, SUB, LANES)
    dma = pltpu.SemaphoreType.DMA
    held = pl.BlockSpec(memory_space=pltpu.HBM)
    scalar = pl.BlockSpec(memory_space=pltpu.SMEM)
    vector = pl.BlockSpec(memory_space=pltpu.VMEM)
    one = jax.ShapeDtypeStruct((1,), jnp.float32)
    return pl.pallas_call(
        functools.partial(kernel, n_seg, n_tile, 1.0 / cells, 1.0 / (2 * cells)),
        out_shape=(jax.ShapeDtypeStruct(base.shape, jnp.float32), one, one),
        in_specs=[held, held, scalar, scalar, held],
        out_specs=(vector, scalar, scalar),
        scratch_shapes=[wide] * 6 + [plain] * 5 + [
            pltpu.VMEM(part, jnp.float32),
            pltpu.VMEM((n_tile, *part), jnp.float32),
            pltpu.VMEM((n_seg, *part), jnp.float32),
            pltpu.VMEM((1, width), jnp.float32),
            dma((3,)), dma((12,)), dma((12,)), dma((blocks,)), dma((blocks,)), dma((blocks,)), dma((blocks,)),
            dma((2, n_tile)), dma((n_seg,)), dma((n_seg,)),
        ],
        compiler_params=pltpu.CompilerParams(
            collective_id=0, has_side_effects=True, vmem_limit_bytes=62 * 1024 * 1024
        ),
    )(base, direction, step_time, step_change, forcing)


def solution(mesh):
    spec = P(("orbit", "seg"), None, "tile", None)
    return jax.shard_map(
        functools.partial(body, mesh.shape["seg"], mesh.shape["tile"]),
        mesh=mesh,
        in_specs=(spec, spec, P("orbit"), P("orbit")),
        out_specs=(spec, P("orbit"), P("orbit")),
        check_vma=False,
    )
```

```python
import functools
import math

import jax
import jax.numpy as jnp
import numpy as np
from jax import lax
from jax.experimental import pallas as pl
from jax.experimental.pallas import tpu as pltpu
from jax.sharding import PartitionSpec as P

K_FORCE = 4

VISC = 0.5

MESH = pl.DeviceIdType.MESH
LANES = 128
SUB = 8
CHUNK = 256


class Window:
    def __init__(self, ref, comp, col, width):
        full, rows = ref.shape[-1], ref.shape[-2] - 2 * SUB
        here = pl.ds(pl.multiple_of(col, LANES), width)
        before = pl.multiple_of(lax.rem(col + (full - LANES), full), LANES)
        after = pl.multiple_of(lax.rem(col + width, full), LANES)
        own = pl.ds(SUB, rows)
        self.mid = ref[comp, own, here]
        self.up = ref[comp, pl.ds(SUB - 1, rows), here]
        self.down = ref[comp, pl.ds(SUB + 1, rows), here]
        wide = jnp.concatenate(
            [ref[comp, own, pl.ds(before, LANES)], self.mid, ref[comp, own, pl.ds(after, LANES)]], axis=1
        )
        self.left = pltpu.roll(wide, 1, 1)[:, LANES : LANES + width]
        self.right = pltpu.roll(wide, wide.shape[1] - 1, 1)[:, LANES : LANES + width]

    def dx(self):
        return (self.down - self.up) * 0.5

    def dy(self):
        return (self.right - self.left) * 0.5

    def lap(self):
        return self.down + self.up + self.right + self.left - 4.0 * self.mid


def windows(ref, col, width):
    return Window(ref, 0, col, width), Window(ref, 1, col, width)


def rate_and_tangent(b, p, forcing, substep, change):
    rates, images = [], []
    for c in range(2):
        gx, gy = b[c].dx(), b[c].dy()
        rate = -(b[0].mid * gx + b[1].mid * gy) + VISC * b[c].lap()
        if c == 0:
            rate = rate + forcing
        move = -b[0].mid * p[c].dx() - b[1].mid * p[c].dy() - p[0].mid * gx - p[1].mid * gy
        move = move + VISC * p[c].lap()
        rates.append(rate)
        images.append(p[c].mid + substep * move + change * rate)
    return rates, images


def adjoint(b, q, substep):
    outs = []
    for c in range(2):
        flux_x = (b[0].down * q[c].down - b[0].up * q[c].up) * 0.5
        flux_y = (b[1].right * q[c].right - b[1].left * q[c].left) * 0.5
        if c == 0:
            cross = b[0].dx() * q[0].mid + b[1].dx() * q[1].mid
        else:
            cross = b[0].dy() * q[0].mid + b[1].dy() * q[1].mid
        outs.append(q[c].mid + substep * (flux_x + flux_y + VISC * q[c].lap() - cross))
    return outs


def folded(x):
    total = None
    for i in range(x.shape[0] // SUB):
        for k in range(x.shape[1] // LANES):
            part = x[i * SUB : (i + 1) * SUB, k * LANES : (k + 1) * LANES]
            total = part if total is None else total + part
    return total


def kernel(
    n_seg, n_tile, scale_time, scale_square,
    base_hbm, pert_hbm, time_ref, change_ref, force_hbm,
    grad_ref, step_ref, square_ref,
    base, pert, mid, pone, res, adj, rate0, rate1, image, ahead, behind, sums, pair, slots, force_ref,
    local_sem, edge_send, edge_recv, ahead_send, ahead_recv, behind_send, behind_recv,
    pair_sem, slot_send, slot_recv,
):
    seg = lax.axis_index("seg")
    tile = lax.axis_index("tile")
    seg_next, seg_prev = lax.rem(seg + 1, n_seg), lax.rem(seg + n_seg - 1, n_seg)
    tile_next, tile_prev = lax.rem(tile + 1, n_tile), lax.rem(tile + n_tile - 1, n_tile)
    rows, width = pert_hbm.shape[2], pert_hbm.shape[3]
    blocks = rows // SUB
    chunk = min(CHUNK, width)
    substep, change = time_ref[0], change_ref[0]

    barrier = pltpu.get_barrier_semaphore()
    for k in range(1, n_seg):
        pl.semaphore_signal(barrier, inc=1, device_id={"seg": lax.rem(seg + k, n_seg)}, device_id_type=MESH)
    for k in range(1, n_tile):
        pl.semaphore_signal(barrier, inc=1, device_id={"tile": lax.rem(tile + k, n_tile)}, device_id_type=MESH)

    own = pl.ds(SUB, rows)
    loads = [
        pltpu.make_async_copy(base_hbm.at[0], base.at[:, own, :], local_sem.at[0]),
        pltpu.make_async_copy(force_hbm, force_ref, local_sem.at[2]),
        pltpu.make_async_copy(pert_hbm.at[0], pert.at[:, own, :], local_sem.at[1]),
    ]
    for copy in loads:
        copy.start()
    pl.semaphore_wait(barrier, n_seg - 1 + n_tile - 1)

    def edges(first, last, field, at):
        down = pltpu.make_async_remote_copy(
            src_ref=last, dst_ref=field.at[:, pl.ds(SUB - 1, 1), :], send_sem=edge_send.at[at], recv_sem=edge_recv.at[at],
            device_id={"tile": tile_next}, device_id_type=MESH)
        up = pltpu.make_async_remote_copy(
            src_ref=first, dst_ref=field.at[:, pl.ds(SUB + rows, 1), :], send_sem=edge_send.at[at + 1],
            recv_sem=edge_recv.at[at + 1], device_id={"tile": tile_prev}, device_id_type=MESH)
        down.start()
        up.start()
        return [down, up]

    def field_edges(field, at):
        return edges(field.at[:, pl.ds(SUB, 1), :], field.at[:, pl.ds(SUB + rows - 1, 1), :], field, at)

    def hbm_edges(field_hbm, field, at):
        return edges(field_hbm.at[0, :, pl.ds(0, 1), :], field_hbm.at[0, :, pl.ds(rows - 1, 1), :], field, at)

    pending = hbm_edges(base_hbm, base, 0) + hbm_edges(pert_hbm, pert, 2)
    aheads = []
    for k in range(blocks):
        part = pl.ds(k * SUB, SUB)
        copy = pltpu.make_async_remote_copy(
            src_ref=pert_hbm.at[0, :, part, :], dst_ref=ahead.at[:, part, :], send_sem=ahead_send.at[k],
            recv_sem=ahead_recv.at[k], device_id={"seg": seg_prev}, device_id_type=MESH)
        if k < blocks // 2:
            copy.start()
        aheads.append(copy)

    def sweep(step):
        def one(j, _):
            step(pl.multiple_of(j * chunk, chunk))
            return 0

        lax.fori_loop(0, width // chunk, one, 0)

    sums[...] = jnp.zeros_like(sums)
    for copy in loads:
        copy.wait()
    for copy in pending:
        copy.wait()

    def first_step(col):
        b, p = windows(base, col, chunk), windows(pert, col, chunk)
        forcing = force_ref[:, pl.ds(col, chunk)]
        rates, images = rate_and_tangent(b, p, forcing, substep, change)
        for c in range(2):
            rate0[c, :, pl.ds(col, chunk)] = rates[c]
            mid[c, own, pl.ds(col, chunk)] = b[c].mid + substep * rates[c]
            pone[c, own, pl.ds(col, chunk)] = images[c]

    sweep(first_step)
    pending = field_edges(mid, 4) + field_edges(pone, 6)
    for copy in aheads[blocks // 2 :]:
        copy.start()
    for copy in pending:
        copy.wait()

    def second_step(col):
        b, p = windows(mid, col, chunk), windows(pone, col, chunk)
        forcing = force_ref[:, pl.ds(col, chunk)]
        rates, images = rate_and_tangent(b, p, forcing, substep, change)
        for c in range(2):
            rate1[c, :, pl.ds(col, chunk)] = rates[c]
            image[c, :, pl.ds(col, chunk)] = images[c]

    sweep(second_step)
    behinds = []
    for k in range(blocks):
        part = pl.ds(k * SUB, SUB)
        copy = pltpu.make_async_remote_copy(
            src_ref=image.at[:, part, :], dst_ref=behind.at[:, part, :], send_sem=behind_send.at[k],
            recv_sem=behind_recv.at[k], device_id={"seg": seg_next}, device_id_type=MESH)
        behinds.append(copy)

    for k in range(blocks):
        aheads[k].wait_recv()
        part, wide_part = pl.ds(k * SUB, SUB), pl.ds((k + 1) * SUB, SUB)

        def residual_step(col):
            for c in range(2):
                value = image[c, part, pl.ds(col, chunk)] - ahead[c, part, pl.ds(col, chunk)]
                res[c, wide_part, pl.ds(col, chunk)] = value
                sums[0] += folded(value * value)
                sums[1] += folded(rate1[c, part, pl.ds(col, chunk)] * value)

        sweep(residual_step)
    pending = field_edges(res, 8)
    quarter = max(blocks // 4, 1)
    for copy in behinds[: 2 * quarter]:
        copy.start()
    for copy in pending + aheads:
        copy.wait_send()
    for copy in pending:
        copy.wait_recv()

    def adjoint_one(col):
        outs = adjoint(windows(mid, col, chunk), windows(res, col, chunk), substep)
        for c in range(2):
            adj[c, own, pl.ds(col, chunk)] = outs[c]
            sums[1] += folded(rate0[c, :, pl.ds(col, chunk)] * outs[c])

    sweep(adjoint_one)
    pending = field_edges(adj, 10)
    shares = []
    for k in range(1, n_tile):
        copy = pltpu.make_async_remote_copy(
            src_ref=sums, dst_ref=pair.at[tile], send_sem=pair_sem.at[0, k], recv_sem=pair_sem.at[1, tile],
            device_id={"tile": lax.rem(tile + k, n_tile)}, device_id_type=MESH)
        copy.start()
        shares.append(copy)
    for copy in behinds[2 * quarter : 3 * quarter]:
        copy.start()
    for copy in pending:
        copy.wait()

    for copy in shares:
        copy.wait_send()
    for k in range(1, n_tile):
        source = lax.rem(tile + k, n_tile)
        pltpu.make_async_remote_copy(
            src_ref=sums, dst_ref=pair.at[source], send_sem=pair_sem.at[0, k], recv_sem=pair_sem.at[1, source],
            device_id={"tile": source}, device_id_type=MESH).wait_recv()
    pair[tile] = sums[...]
    both = pair[0]
    for k in range(1, n_tile):
        both = both + pair[k]
    slots[seg] = both
    sends = []
    for k in range(1, n_seg):
        copy = pltpu.make_async_remote_copy(
            src_ref=slots.at[seg], dst_ref=slots.at[seg], send_sem=slot_send.at[k], recv_sem=slot_recv.at[seg],
            device_id={"seg": lax.rem(seg + k, n_seg)}, device_id_type=MESH)
        copy.start()
        sends.append(copy)
    for copy in behinds[3 * quarter :]:
        copy.start()

    def adjoint_zero(col):
        outs = adjoint(windows(base, col, chunk), windows(adj, col, chunk), substep)
        for c in range(2):
            pone[c, own, pl.ds(col, chunk)] = outs[c] + pert[c, own, pl.ds(col, chunk)]

    sweep(adjoint_zero)

    for copy in sends:
        copy.wait_send()
    for k in range(1, n_seg):
        source = lax.rem(seg + k, n_seg)
        pltpu.make_async_remote_copy(
            src_ref=slots.at[source], dst_ref=slots.at[source], send_sem=slot_send.at[k],
            recv_sem=slot_recv.at[source], device_id={"seg": source}, device_id_type=MESH).wait_recv()
    total = slots[0]
    for k in range(1, n_seg):
        total = total + slots[k]
    square_ref[0] = jnp.sum(total[0]) * scale_square
    step_ref[0] = jnp.sum(total[1]) * scale_time

    for k in range(blocks):
        behinds[k].wait_recv()
        part, wide_part = pl.ds(k * SUB, SUB), pl.ds((k + 1) * SUB, SUB)

        def last_step(col):
            for c in range(2):
                here = pl.ds(col, chunk)
                grad_ref[0, c, part, here] = pone[c, wide_part, here] - behind[c, part, here]

        sweep(last_step)
    for copy in behinds:
        copy.wait_send()


def body(n_seg, n_tile, base, direction, step_time, step_change):
    _, comps, rows, width = base.shape
    cells = rows * width * n_seg * n_tile
    forcing = np.sin(2.0 * math.pi * K_FORCE * np.arange(width) / width).astype(np.float32)[None]
    blocks = rows // SUB
    wide = pltpu.VMEM((comps, rows + 2 * SUB, width), jnp.float32)
    plain = pltpu.VMEM((comps, rows, width), jnp.float32)
    part = (2, SUB, LANES)
    dma = pltpu.SemaphoreType.DMA
    held = pl.BlockSpec(memory_space=pltpu.HBM)
    scalar = pl.BlockSpec(memory_space=pltpu.SMEM)
    vector = pl.BlockSpec(memory_space=pltpu.VMEM)
    one = jax.ShapeDtypeStruct((1,), jnp.float32)
    return pl.pallas_call(
        functools.partial(kernel, n_seg, n_tile, 1.0 / cells, 1.0 / (2 * cells)),
        out_shape=(jax.ShapeDtypeStruct(base.shape, jnp.float32), one, one),
        in_specs=[held, held, scalar, scalar, held],
        out_specs=(vector, scalar, scalar),
        scratch_shapes=[wide] * 6 + [plain] * 5 + [
            pltpu.VMEM(part, jnp.float32),
            pltpu.VMEM((n_tile, *part), jnp.float32),
            pltpu.VMEM((n_seg, *part), jnp.float32),
            pltpu.VMEM((1, width), jnp.float32),
            dma((3,)), dma((12,)), dma((12,)), dma((blocks,)), dma((blocks,)), dma((blocks,)), dma((blocks,)),
            dma((2, n_tile)), dma((n_seg,)), dma((n_seg,)),
        ],
        compiler_params=pltpu.CompilerParams(
            collective_id=0, has_side_effects=True, vmem_limit_bytes=62 * 1024 * 1024
        ),
    )(base, direction, step_time, step_change, forcing)


def solution(mesh):
    spec = P(("orbit", "seg"), None, "tile", None)
    return jax.shard_map(
        functools.partial(body, mesh.shape["seg"], mesh.shape["tile"]),
        mesh=mesh,
        in_specs=(spec, spec, P("orbit"), P("orbit")),
        out_specs=(spec, P("orbit"), P("orbit")),
        check_vma=False,
    )
```
